32 devices in a mesh: row: 8 (over z, y), col: 4 (over x, core).
Axes of the slice: x: 2, y: 2, z: 4, core: 2. Of those that a mesh axis runs over, the one named last changes fastest.
Arguments:
- patches: bfloat16 [16, 8, 8, 8192], P('row', None, None, 'col'), may hold values from -6 to 6
- out_grad: bfloat16 [16, 8, 8, 8192], P('row', None, None, 'col'), may hold values from -6 to 6
- conv_kernel: float32 [3, 3, 3, 8192], P(None, None, None, 'col'), may hold values from -1.25 to 1.25
- saved_gate: bfloat16 [1024, 14336], P('col', 'row'), may hold values from -6 to 6
- saved_up: bfloat16 [1024, 14336], P('col', 'row'), may hold values from -6 to 6
- w_gate: bfloat16 [8192, 14336], P('col', 'row'), may hold values from -0.0625 to 0.0625
- w_up: bfloat16 [8192, 14336], P('col', 'row'), may hold values from -0.0625 to 0.0625
- w_down: bfloat16 [14336, 8192], P('row', 'col'), may hold values from -0.046875 to 0.046875
Outputs:
- patch_grad: bfloat16 [16, 8, 8, 8192], P('row', None, None, 'col')
- kernel_grad: float32 [3, 3, 3, 8192], P(None, None, None, 'col')
- gate_wgrad: bfloat16 [8192, 14336], P('col', 'row')
- up_wgrad: bfloat16 [8192, 14336], P('col', 'row')
- down_wgrad: bfloat16 [14336, 8192], P('row', 'col')
The draws below stay inside these ranges and needn't reach their ends.
All inputs are finite; a program needn't handle non-finite values.
Results may differ from the reference program's by a relative error of at most 0.02.
Values may be sent and summed in bfloat16 or wider, within the bound.
No kernel may reach another device: no remote copies, remote signals or barrier semaphores. Data moves between devices by JAX's collectives and lax.ppermute only.
A program may use at most 128 MiB of HBM per device.

```python
import jax
import jax.numpy as jnp
from jax import lax

D = 8192
FF = 14336
YD = 8
XD = 8
ZD = 16
TOKENS = 1024
N_ROW = 8
N_COL = 4


def block_levels(stream_key, extent, cuts, least, largest):
    loudness, own = 1.0, jax.random.fold_in(stream_key, 6)
    for axis_at, shards_of in cuts:
        heights = jnp.exp(jax.random.uniform(jax.random.fold_in(own, axis_at), (shards_of,), jnp.float32, least / len(cuts), largest / len(cuts)))
        loudness = loudness * jnp.repeat(heights, extent[axis_at] // shards_of).reshape([-1 if axis == axis_at else 1 for axis in range(len(extent))])
    return loudness


def gaussian(key, extent, scale, bound, pieces=(), dtype=jnp.bfloat16):
    loudness = block_levels(key, extent, pieces, -0.22, 0.18) if pieces else 1.0
    entries = jax.random.normal(key, extent, jnp.float32) * scale * loudness
    return jnp.minimum(jnp.maximum(entries, -bound), bound).astype(dtype)


def setup_inputs(seed: int = 0) -> dict:
    keys = jax.random.split(jax.random.key(seed), 9)
    patches = gaussian(keys[0], (ZD, YD, XD, D), 1.0, 6.0, ((0, 8), (3, 4)))
    out_grad = gaussian(keys[1], (ZD, YD, XD, D), 0.5, 6.0, ((0, 8), (3, 4)))
    conv_kernel = gaussian(keys[2], (3, 3, 3, D), 27 ** -0.5, 1.25, ((3, 4),), jnp.float32)
    saved_gate = gaussian(keys[3], (TOKENS, FF), 1.0, 6.0, ((0, 4), (1, 8)))
    saved_up = gaussian(keys[4], (TOKENS, FF), 1.0, 6.0, ((0, 4), (1, 8)))
    w_gate = gaussian(keys[5], (D, FF), D ** -0.5, 0.0625, ((0, 4), (1, 8)))
    w_up = gaussian(keys[6], (D, FF), D ** -0.5, 0.0625, ((0, 4), (1, 8)))
    w_down = gaussian(keys[7], (FF, D), FF ** -0.5, 0.046875, ((0, 8), (1, 4)))
    return {"patches": patches, "out_grad": out_grad, "conv_kernel": conv_kernel, "saved_gate": saved_gate, "saved_up": saved_up, "w_gate": w_gate, "w_up": w_up, "w_down": w_down}


def correlate(framed, kernel, flipped):
    planes = framed.shape[0] - 2
    height = framed.shape[1] - 2
    breadth = framed.shape[2] - 2
    summed = jnp.zeros((planes, height, breadth, framed.shape[3]), jnp.float32)
    for along_z in range(3):
        for along_y in range(3):
            for along_x in range(3):
                if flipped:
                    lead_z, lead_y, lead_x = 2 - along_z, 2 - along_y, 2 - along_x
                else:
                    lead_z, lead_y, lead_x = along_z, along_y, along_x
                window = framed[lead_z:lead_z + planes, lead_y:lead_y + height, lead_x:lead_x + breadth]
                summed = summed + kernel[along_z, along_y, along_x] * window
    return summed


def frame(field):
    return jnp.pad(field, ((1, 1), (1, 1), (1, 1), (0, 0)))


def tap_sums(grads, framed):
    planes, height, breadth = grads.shape[0], grads.shape[1], grads.shape[2]
    layers = []
    for along_z in range(3):
        for along_y in range(3):
            for along_x in range(3):
                window = framed[along_z:along_z + planes, along_y:along_y + height, along_x:along_x + breadth]
                layers.append(jnp.sum(grads * window, axis=(0, 1, 2)))
    return jnp.stack(layers).reshape(3, 3, 3, grads.shape[3])


def reference(patches, out_grad, conv_kernel, saved_gate, saved_up, w_gate, w_up, w_down):
    patch_f = patches.astype(jnp.float32)
    framed_in = frame(patch_f)
    mixed_in = (patch_f + correlate(framed_in, conv_kernel, False)).astype(jnp.bfloat16)
    flat_in = mixed_in.reshape(TOKENS, D)
    flat_grad = out_grad.reshape(TOKENS, D)
    block_width = D // N_COL
    hidden_grad = jnp.zeros((TOKENS, FF), jnp.float32)
    for block in range(N_COL):
        grad_block = flat_grad[:, block * block_width:(block + 1) * block_width]
        down_block = w_down[:, block * block_width:(block + 1) * block_width]
        partial_value = lax.dot_general(grad_block, down_block, (((1,), (1,)), ((), ())), preferred_element_type=jnp.float32)
        rounded = lax.optimization_barrier(partial_value.astype(jnp.bfloat16))
        hidden_grad = hidden_grad + rounded.astype(jnp.float32)
    gate_f = saved_gate.astype(jnp.float32)
    up_f = saved_up.astype(jnp.float32)
    sigmoid_g = jax.nn.sigmoid(gate_f)
    silu_g = gate_f * sigmoid_g
    hidden_act = (silu_g * up_f).astype(jnp.bfloat16)
    gate_grad = (hidden_grad * up_f * sigmoid_g * (1.0 + gate_f * (1.0 - sigmoid_g))).astype(jnp.bfloat16)
    up_grad = (hidden_grad * silu_g).astype(jnp.bfloat16)
    contract_rows = (((0,), (0,)), ((), ()))
    down_wgrad = lax.dot_general(hidden_act, flat_grad, contract_rows, preferred_element_type=jnp.float32).astype(jnp.bfloat16)
    gate_wgrad = lax.dot_general(flat_in, gate_grad, contract_rows, preferred_element_type=jnp.float32).astype(jnp.bfloat16)
    up_wgrad = lax.dot_general(flat_in, up_grad, contract_rows, preferred_element_type=jnp.float32).astype(jnp.bfloat16)
    contract_cols = (((1,), (1,)), ((), ()))
    unit_width = FF // N_ROW
    total_grad = flat_grad.astype(jnp.float32)
    for block in range(N_ROW):
        lower = block * unit_width
        upper = (block + 1) * unit_width
        term = lax.dot_general(gate_grad[:, lower:upper], w_gate[:, lower:upper], contract_cols, preferred_element_type=jnp.float32)
        term = term + lax.dot_general(up_grad[:, lower:upper], w_up[:, lower:upper], contract_cols, preferred_element_type=jnp.float32)
        rounded = lax.optimization_barrier(term.astype(jnp.bfloat16))
        total_grad = total_grad + rounded.astype(jnp.float32)
    total_grad = total_grad.reshape(ZD, YD, XD, D)
    patch_grad = (total_grad + correlate(frame(total_grad), conv_kernel, True)).astype(jnp.bfloat16)
    kernel_grad = tap_sums(total_grad, framed_in)
    return (patch_grad, kernel_grad, gate_wgrad, up_wgrad, down_wgrad)
```

```python
import jax
import jax.numpy as jnp
from jax import lax
from jax.sharding import PartitionSpec as P

F32 = jnp.float32
BF16 = jnp.bfloat16
CONTRACT_COLS = (((1,), (1,)), ((), ()))
CONTRACT_ROWS = (((0,), (0,)), ((), ()))


def dot(a, b, dims):
    return lax.dot_general(a, b, dims, preferred_element_type=F32)


def after(value, *earlier):
    return lax.optimization_barrier((value, *earlier))[0]


def ring_order(peers):
    return list(range(0, peers, 2)) + list(range(1, peers, 2))[::-1]


class Ring:
    def __init__(self, axis):
        self.axis = axis
        self.size = lax.axis_size(axis)
        self.order = ring_order(self.size)
        self.up = [(self.order[i], self.order[(i + 1) % self.size]) for i in range(self.size)]
        self.down = [(j, i) for i, j in self.up]
        place = [self.order.index(i) for i in range(self.size)]
        self.place = jnp.array(place, jnp.int32)[lax.axis_index(axis)]

    def index_at(self, distance):
        spot = lax.rem(self.place + (distance + self.size), self.size)
        return jnp.array(self.order, jnp.int32)[spot]

    def to_up(self, x):
        return lax.ppermute(x, self.axis, self.up)

    def to_down(self, x):
        return lax.ppermute(x, self.axis, self.down)

    def gather(self, x):
        half, rows = (self.size // 2, x.shape[0])
        blocks = {0: x}
        from_below, from_above = (x, x)
        for step in range(1, half):
            from_below, from_above = (self.to_up(from_below), self.to_down(from_above))
            blocks[-step], blocks[step] = (from_below, from_above)
        first = self.to_up(from_below[: rows // 2])
        second = self.to_down(from_above[rows // 2 :])
        blocks[half] = jnp.concatenate([first, second], axis=0)
        return blocks


def padded(x, axis):
    peers = lax.axis_size(axis)
    up = [(i, (i + 1) % peers) for i in range(peers - 1)]
    down = [(j, i) for i, j in up]
    before = lax.ppermute(x[-1:], axis, up)
    later = lax.ppermute(x[:1], axis, down)
    return jnp.concatenate([before, x, later], axis=0)


def correlate(framed, kernel, flipped):
    planes, height, breadth = (n - 2 for n in framed.shape[:3])
    summed = jnp.zeros((planes, height, breadth, framed.shape[3]), F32)
    for along_z in range(3):
        for along_y in range(3):
            for along_x in range(3):
                if flipped:
                    lead_z, lead_y, lead_x = (2 - along_z, 2 - along_y, 2 - along_x)
                else:
                    lead_z, lead_y, lead_x = (along_z, along_y, along_x)
                window = framed[
                    lead_z : lead_z + planes, lead_y : lead_y + height, lead_x : lead_x + breadth
                ]
                summed = summed + kernel[along_z, along_y, along_x] * window
    return summed


def frame_sides(field):
    return jnp.pad(field, ((0, 0), (1, 1), (1, 1), (0, 0)))


def tap_sums(grads, framed):
    planes, height, breadth = grads.shape[:3]
    layers = []
    for along_z in range(3):
        for along_y in range(3):
            for along_x in range(3):
                window = framed[
                    along_z : along_z + planes,
                    along_y : along_y + height,
                    along_x : along_x + breadth,
                ]
                layers.append(jnp.sum(grads * window, axis=(0, 1, 2)))
    return jnp.stack(layers)


def sum_over(x, axis):
    peers = lax.axis_size(axis)
    if peers & (peers - 1):
        return lax.psum(x.astype(BF16), axis).astype(F32)
    reach = 1
    while reach < peers:
        mine = x.astype(BF16)
        theirs = lax.ppermute(mine, axis, [(i, i ^ reach) for i in range(peers)])
        x = mine.astype(F32) + theirs.astype(F32)
        reach *= 2
    return x


def swap_cores(x):
    peers = lax.axis_size("col")
    return lax.ppermute(x, "col", [(i, i ^ 1) for i in range(peers)])


def shift_chips(x, count):
    peers = lax.axis_size("col")
    return lax.ppermute(x, "col", [(i, (i + 2 * count) % peers) for i in range(peers)])


def gather_cols(x):
    chips = lax.axis_size("col") // 2
    mine = [x] + [shift_chips(x, k) for k in range(1, chips)]
    other = [swap_cores(block) for block in mine]
    return jnp.concatenate(mine + other, axis=0)


def col_place(block):
    chips = lax.axis_size("col") // 2
    me = lax.axis_index("col")
    chip_gap = lax.rem(me // 2 - block // 2 + chips, chips)
    other = jnp.where(lax.rem(me, 2) == lax.rem(block, 2), 0, 1)
    return other * chips + chip_gap


def sum_cols(x):
    rows, chips = (x.shape[0] // 2, lax.axis_size("col") // 2)
    core = lax.rem(lax.axis_index("col"), 2)
    x = x.astype(BF16)
    keep = jnp.where(core == 0, x[:rows], x[rows:])
    give = jnp.where(core == 0, x[rows:], x[:rows])
    pair = (keep.astype(F32) + swap_cores(give).astype(F32)).astype(BF16)
    whole = pair.astype(F32)
    for k in range(1, chips):
        whole = whole + shift_chips(pair, k).astype(F32)
    whole = whole.astype(BF16)
    theirs = swap_cores(whole)
    first = jnp.where(core == 0, whole, theirs)
    second = jnp.where(core == 0, theirs, whole)
    return jnp.concatenate([first, second], axis=0)


def body(patches, out_grad, conv_kernel, saved_gate, saved_up, w_gate, w_up, w_down):
    planes, height, breadth, features = patches.shape
    ring = Ring("row")
    half = ring.size // 2
    rows = planes * height * breadth
    flat_grad = out_grad.reshape(rows, features)

    rimmed = padded(patches, "row")
    grad_blocks = ring.gather(flat_grad)
    gate_all, up_all = (gather_cols(saved_gate), gather_cols(saved_up))
    col_rows = saved_gate.shape[0]

    def token_rows(x, distance):
        start = ring.index_at(distance) * rows
        at = col_place(start // col_rows) * col_rows + lax.rem(start, col_rows)
        return lax.dynamic_slice_in_dim(x, at, rows, axis=0)

    framed_in = frame_sides(rimmed.astype(F32))
    mixed_in = (patches.astype(F32) + correlate(framed_in, conv_kernel, False)).astype(BF16)
    mixed_in = after(mixed_in.reshape(rows, features), grad_blocks[half])
    mixed_blocks = ring.gather(mixed_in)

    groups = [[half], [half - 1, 1 - half]]
    groups += [[d, -d] for d in range(half - 2, 0, -1)] + [[0]]
    order = [d for group in groups for d in group]

    hidden, gate_grads, up_grads, gates, ups = ({}, {}, {}, {}, {})
    for group in groups:
        block = jnp.concatenate([grad_blocks[d] for d in group], axis=0)
        hidden[group[0]] = dot(block, w_down, CONTRACT_COLS).astype(BF16)

    sent_up, sent_down = (None, None)
    for group in groups:
        total = sum_cols(hidden[group[0]]).astype(F32)
        gate = jnp.concatenate([token_rows(gate_all, d) for d in group], axis=0).astype(F32)
        up = jnp.concatenate([token_rows(up_all, d) for d in group], axis=0).astype(F32)
        sig = jax.nn.sigmoid(gate)
        silu = gate * sig
        hidden[group[0]] = (silu * up).astype(BF16)
        gate_grad = (total * up * sig * (1.0 + gate * (1.0 - sig))).astype(BF16)
        up_grad = (total * silu).astype(BF16)
        gate_grad, up_grad = lax.optimization_barrier((gate_grad, up_grad))
        gate_grads[group[0]], up_grads[group[0]] = (gate_grad, up_grad)
        term = dot(gate_grad, w_gate, CONTRACT_COLS) + dot(up_grad, w_up, CONTRACT_COLS)
        if group[0] == half:
            term = term.astype(BF16)
            sent_up = ring.to_up(term[: rows // 2])
            sent_down = ring.to_down(term[rows // 2 :])
        elif group[0] == 0:
            mlp_grad = term + sent_up.astype(F32) + sent_down.astype(F32)
        else:
            going_up, going_down = (term[:rows], term[rows:])
            if group[0] == half - 1:
                going_up = going_up + jnp.pad(sent_up.astype(F32), ((0, rows // 2), (0, 0)))
                going_down = going_down + jnp.pad(sent_down.astype(F32), ((rows // 2, 0), (0, 0)))
            else:
                going_up = going_up + sent_up.astype(F32)
                going_down = going_down + sent_down.astype(F32)
            sent_up = ring.to_up(going_up.astype(BF16))
            sent_down = ring.to_down(going_down.astype(BF16))

    def stacked(parts):
        return jnp.concatenate([parts[g[0]] for g in groups], axis=0)

    def blocks_in_order(parts):
        return jnp.concatenate([parts[d] for d in order], axis=0)

    hidden_all, gate_grad_all, up_grad_all, grad_all, mixed_all = lax.optimization_barrier(
        (
            stacked(hidden),
            stacked(gate_grads),
            stacked(up_grads),
            blocks_in_order(grad_blocks),
            blocks_in_order(mixed_blocks),
        )
    )
    down_wgrad = dot(hidden_all, grad_all, CONTRACT_ROWS).astype(BF16)
    gate_wgrad = dot(mixed_all, gate_grad_all, CONTRACT_ROWS).astype(BF16)
    up_wgrad = dot(mixed_all, up_grad_all, CONTRACT_ROWS).astype(BF16)

    total_grad = out_grad.astype(F32) + mlp_grad.reshape(planes, height, breadth, features)
    grad_rimmed = padded(total_grad.astype(BF16), "row").astype(F32)
    patch_grad = (total_grad + correlate(frame_sides(grad_rimmed), conv_kernel, True)).astype(BF16)
    kernel_grad = sum_over(tap_sums(total_grad, framed_in), "row").reshape(conv_kernel.shape)
    return (patch_grad, kernel_grad, gate_wgrad, up_wgrad, down_wgrad)


def solution(mesh):
    return jax.shard_map(
        body,
        mesh=mesh,
        in_specs=(
            P("row", None, None, "col"),
            P("row", None, None, "col"),
            P(None, None, None, "col"),
            P("col", "row"),
            P("col", "row"),
            P("col", "row"),
            P("col", "row"),
            P("row", "col"),
        ),
        out_specs=(
            P("row", None, None, "col"),
            P(None, None, None, "col"),
            P("col", "row"),
            P("col", "row"),
            P("row", "col"),
        ),
        check_vma=False,
    )
```

```python
import functools

import jax
import jax.numpy as jnp
import numpy as np
from jax import lax
from jax.experimental import pallas as pl
from jax.experimental.pallas import tpu as pltpu
from jax.sharding import PartitionSpec as P

F32 = jnp.float32
BF16 = jnp.bfloat16
CONTRACT_COLS = (((1,), (1,)), ((), ()))
CONTRACT_ROWS = (((0,), (0,)), ((), ()))


def dot(a, b, dims):
    return lax.dot_general(a, b, dims, preferred_element_type=F32)


def after(values, *earlier):
    return lax.optimization_barrier((values, earlier))[0]


def ring_order(peers):
    return list(range(0, peers, 2)) + list(range(1, peers, 2))[::-1]


class Ring:
    def __init__(self, axis):
        self.axis = axis
        self.size = lax.axis_size(axis)
        self.order = ring_order(self.size)
        self.up = [(self.order[i], self.order[(i + 1) % self.size]) for i in range(self.size)]
        self.down = [(j, i) for i, j in self.up]

    def neighbour(self, index, distance):
        return self.order[(self.order.index(index) + distance) % self.size]

    def to_up(self, x):
        return lax.ppermute(x, self.axis, self.up)

    def to_down(self, x):
        return lax.ppermute(x, self.axis, self.down)


def neighbour_planes(x, axis):
    peers = lax.axis_size(axis)
    up = [(i, (i + 1) % peers) for i in range(peers - 1)]
    down = [(j, i) for i, j in up]
    return (lax.ppermute(x[-1:], axis, up), lax.ppermute(x[:1], axis, down))


def correlate(framed, kernel, flipped):
    planes, height, breadth = (n - 2 for n in framed.shape[:3])
    summed = jnp.zeros((planes, height, breadth, framed.shape[3]), F32)
    for along_z in range(3):
        for along_y in range(3):
            for along_x in range(3):
                if flipped:
                    lead_z, lead_y, lead_x = (2 - along_z, 2 - along_y, 2 - along_x)
                else:
                    lead_z, lead_y, lead_x = (along_z, along_y, along_x)
                window = framed[
                    lead_z : lead_z + planes, lead_y : lead_y + height, lead_x : lead_x + breadth
                ]
                summed = summed + kernel[along_z, along_y, along_x] * window
    return summed


def frame_sides(field):
    return jnp.pad(field, ((0, 0), (1, 1), (1, 1), (0, 0)))


def tap_sums(grads, framed):
    planes, height, breadth = grads.shape[:3]
    layers = []
    for along_z in range(3):
        for along_y in range(3):
            for along_x in range(3):
                window = framed[
                    along_z : along_z + planes,
                    along_y : along_y + height,
                    along_x : along_x + breadth,
                ]
                layers.append(jnp.sum(grads * window, axis=(0, 1, 2)))
    return jnp.stack(layers)


def sum_over(x, axis):
    peers = lax.axis_size(axis)
    if peers & (peers - 1):
        return lax.psum(x.astype(BF16), axis).astype(F32)
    reach = 1
    while reach < peers:
        mine = x.astype(BF16)

        def partner(gap):
            return lax.ppermute(mine, axis, [(i, i ^ gap) for i in range(peers)]).astype(F32)

        if reach > 1 and reach * 4 <= peers:
            x = (mine.astype(F32) + partner(reach)) + (partner(2 * reach) + partner(3 * reach))
            reach *= 4
        else:
            x = mine.astype(F32) + partner(reach)
            reach *= 2
    return x


def swap_cores(x):
    peers = lax.axis_size("col")
    return lax.ppermute(x, "col", [(i, i ^ 1) for i in range(peers)])


def shift_chips(x, count):
    peers = lax.axis_size("col")
    return lax.ppermute(x, "col", [(i, (i + 2 * count) % peers) for i in range(peers)])


def col_place(me, block, chips):
    other = 0 if me % 2 == block % 2 else 1
    return other * chips + (me // 2 - block // 2) % chips


def piece_table(ring, distances, rows, col_rows, size):
    peers, cols = (ring.size, lax.axis_size("col"))
    table = np.zeros((peers, cols, 2, len(distances) * rows // size), np.int32)
    for row in range(peers):
        starts = [
            ring.neighbour(row, d) * rows + at for d in distances for at in range(0, rows, size)
        ]
        for col in range(cols):
            table[row, col, 0] = [col_place(col, s // col_rows, cols // 2) for s in starts]
            table[row, col, 1] = [s % col_rows for s in starts]
    return jnp.asarray(table)[lax.axis_index("row"), lax.axis_index("col")]


def split_halves(x, core):
    rows = x.shape[0] // 2
    x = x.astype(BF16)
    keep = jnp.where(core == 0, x[:rows], x[rows:])
    give = jnp.where(core == 0, x[rows:], x[:rows])
    return (keep, give)


def add(*terms):
    total = terms[0].astype(F32)
    for term in terms[1:]:
        total = total + term.astype(F32)
    return total.astype(BF16)


LIGHT = pl.CostEstimate(flops=0, bytes_accessed=0, transcendentals=0)


def product_kernel(tokens, weights, refs):
    out = refs[-1]
    total = None
    for n in range(weights):
        rows = [ref[...] for ref in refs[n * tokens : (n + 1) * tokens]]
        rows = rows[0] if tokens == 1 else jnp.concatenate(rows, axis=0)
        term = dot(rows, refs[weights * tokens + n][...], CONTRACT_COLS)
        total = term if total is None else total + term
    out[...] = total.astype(out.dtype)


def product(blocks, weights, name):
    tokens = len(blocks[0])
    rows = sum(block.shape[0] for block in blocks[0])
    wide, depth = weights[0].shape
    tile = next(t for t in (896 if len(weights) == 1 else 512, 512, 256, 128) if wide % t == 0)
    flat = [block for group in blocks for block in group]
    return pl.pallas_call(
        lambda *refs: product_kernel(tokens, len(weights), refs),
        grid=(wide // tile,),
        out_shape=jax.ShapeDtypeStruct((rows, wide), BF16),
        in_specs=[pl.BlockSpec(block.shape, lambda i: (0, 0)) for block in flat]
        + [pl.BlockSpec((tile, depth), lambda i: (i, 0))] * len(weights),
        out_specs=pl.BlockSpec((rows, tile), lambda i: (0, i)),
        compiler_params=pltpu.CompilerParams(vmem_limit_bytes=24 << 20),
        cost_estimate=LIGHT,
        name=name,
    )(*flat, *weights)


def collect_kernel(sources, count, size, where_ref, *refs):
    inputs = (refs[:sources], refs[sources : 2 * sources])
    outputs, sems = (refs[2 * sources : 2 * sources + 2], refs[-1])

    def copies(source, piece, offset):
        place = pl.ds(piece * size, size)
        rows = pl.ds(pl.multiple_of(offset, size), size)
        return [
            pltpu.make_async_copy(inputs[n][source].at[rows], outputs[n].at[place], sems.at[n, piece])
            for n in range(2)
        ]

    for piece in range(count):
        for source in range(sources):

            @pl.when(where_ref[0, piece] == source)
            def _():
                for copy in copies(source, piece, where_ref[1, piece]):
                    copy.start()

    for piece in range(count):
        for copy in copies(0, piece, 0):
            copy.wait()


def collect(gates, ups, where, size):
    sources, count, width = (len(gates), where.shape[1], gates[0].shape[1])
    shape = jax.ShapeDtypeStruct((count * size, width), BF16)
    anywhere = pl.BlockSpec(memory_space=pl.ANY)
    return pl.pallas_call(
        functools.partial(collect_kernel, sources, count, size),
        out_shape=[shape] * 2,
        in_specs=[pl.BlockSpec(memory_space=pltpu.SMEM)] + [anywhere] * (2 * sources),
        out_specs=[anywhere] * 2,
        scratch_shapes=[pltpu.SemaphoreType.DMA((2, count))],
        compiler_params=pltpu.CompilerParams(vmem_limit_bytes=1 << 20),
        cost_estimate=LIGHT,
        name="collect_gate_up",
    )(where, *gates, *ups)


def swiglu_terms(gate, up):
    gate, up = (gate.astype(F32), up.astype(F32))
    sig = jax.nn.sigmoid(gate)
    return (gate, up, sig, gate * sig)


def wgrad_kernel(spans_a, spans_b, tile, a_refs, b_refs, out, a_buf, b_buf, a_sems, b_sems):
    step = pl.program_id(0)
    tiles = a_buf.shape[1] // tile

    def a_copies(t):
        columns = pl.ds(t * tile, tile)
        return [
            pltpu.make_async_copy(
                ref.at[:, columns], a_buf.at[pl.ds(at, rows), columns], a_sems.at[t, n]
            )
            for n, (ref, (at, rows)) in enumerate(zip(a_refs, spans_a))
        ]

    def b_copies():
        return [
            pltpu.make_async_copy(ref, b_buf.at[pl.ds(at, rows)], b_sems.at[n])
            for n, (ref, (at, rows)) in enumerate(zip(b_refs, spans_b))
        ]

    @pl.when(step == 0)
    def _():
        for copy in a_copies(0) + b_copies():
            copy.start()
        for t in range(1, tiles):
            for copy in a_copies(t):
                copy.start()
        for copy in b_copies():
            copy.wait()

    for t in range(tiles):

        @pl.when(step == t)
        def _():
            for copy in a_copies(t):
                copy.wait()
            out[...] = dot(
                a_buf[:, t * tile : (t + 1) * tile], b_buf[...], CONTRACT_ROWS
            ).astype(out.dtype)


def spans(parts):
    at, found = (0, [])
    for part in parts:
        found.append((at, part.shape[0]))
        at += part.shape[0]
    return found


def wgrad(a_parts, b_parts, name):
    depth = sum(part.shape[0] for part in a_parts)
    wide, high = (b_parts[0].shape[1], a_parts[0].shape[1])
    tile = next(t for t in (512, 256, 128) if high % t == 0)
    n_a, n_b = (len(a_parts), len(b_parts))

    def kernel(*refs):
        wgrad_kernel(
            spans(a_parts), spans(b_parts), tile, refs[:n_a], refs[n_a : n_a + n_b], *refs[n_a + n_b :]
        )

    return pl.pallas_call(
        kernel,
        grid=(high // tile,),
        out_shape=pltpu.HBM((high, wide), BF16),
        in_specs=[pl.BlockSpec(memory_space=pltpu.HBM)] * (n_a + n_b),
        out_specs=pl.BlockSpec((tile, wide), lambda i: (i, 0)),
        scratch_shapes=[
            pltpu.VMEM((depth, high), BF16),
            pltpu.VMEM((depth, wide), BF16),
            pltpu.SemaphoreType.DMA((high // tile, n_a)),
            pltpu.SemaphoreType.DMA((n_b,)),
        ],
        compiler_params=pltpu.CompilerParams(vmem_limit_bytes=24 << 20),
        cost_estimate=LIGHT,
        name=name,
    )(*a_parts, *b_parts)


def body(patches, out_grad, conv_kernel, saved_gate, saved_up, w_gate, w_up, w_down):
    planes, height, breadth, features = patches.shape
    ring = Ring("row")
    half = ring.size // 2
    rows = planes * height * breadth
    chips = lax.axis_size("col") // 2
    core = lax.rem(lax.axis_index("col"), 2)
    flat_grad = out_grad.reshape(rows, features)

    far = [half, half - 1, 1 - half]
    near = [1, -1, 0]
    middle = [[d, -d] for d in range(half - 2, 1, -1)]
    groups = [far] + middle + [near]
    order = [d for group in groups for d in group]
    bounds = np.cumsum([0] + [len(group) * rows for group in groups])
    col_rows = saved_gate.shape[0]
    size = int(np.gcd(rows, col_rows))
    where = piece_table(ring, order, rows, col_rows, size)

    def hidden_part(blocks):
        return product([blocks], [w_down], "hidden_grad")

    def pair_sum(partial):
        keep, give = split_halves(partial, core)
        return add(keep, swap_cores(give))

    def chip_shifts(x):
        return [shift_chips(x, k) for k in range(1, chips)]

    keys = [half] + [group[0] for group in middle] + [1]
    sequence = keys[::-1]
    pairs, shifts, halves = ({}, {}, {})

    def sum_group(key):
        whole = add(pairs[key], *shifts[key])
        halves[key] = (whole, swap_cores(whole))
        return whole

    def send_group(key, *earlier):
        shifts[key] = chip_shifts(after(pairs[key], *earlier))

    before, beyond = neighbour_planes(patches, "row")
    grads = {0: flat_grad}
    grads[-1], grads[1] = (ring.to_up(flat_grad), ring.to_down(flat_grad))
    gates = [saved_gate] + chip_shifts(saved_gate)
    ups = [saved_up] + chip_shifts(saved_up)
    hold = ()
    for step in range(2, half + 1):
        back, ahead = after((grads[1 - step], grads[step - 1]), *hold)
        grads[1 - step], grads[step - 1] = (back, ahead)
        if step < half:
            grads[-step], grads[step] = (ring.to_up(back), ring.to_down(ahead))
        else:
            last_up = ring.to_up(back[: rows // 2])
            last_down = ring.to_down(ahead[rows // 2 :])
        if step == 2:
            part = hidden_part([ahead, back, flat_grad])
            pairs[1] = pair_sum(part)
            planes_in, before, beyond = after((patches, before, beyond), part)
            rimmed = jnp.concatenate([before, planes_in, beyond], axis=0)
            framed_in = frame_sides(rimmed.astype(F32))
            mixed_in = planes_in.astype(F32) + correlate(framed_in, conv_kernel, False)
            mixed_in = mixed_in.astype(BF16).reshape(rows, features)
            hold = (part, mixed_in, where)
        elif step < half:
            part = hidden_part([ahead, back])
            pairs[step - 1] = pair_sum(part)
            hold = (part,)
        else:
            far_part = hidden_part([ahead, back])
            gates, ups = after((gates, ups), back, ahead)
            send_group(1, *gates, *ups)
            gates += [swap_cores(x) for x in gates]
            ups += [swap_cores(x) for x in ups]
            hold = (far_part,)
    last_up, last_down = after((last_up, last_down), *hold)
    grads[half] = jnp.concatenate([last_up, last_down], axis=0)
    grad_parts = [grads[d] for d in order]

    gate_grads, up_grads, terms = ({}, {}, {})

    def finish_group(key):
        whole, theirs = halves[key]
        lower, upper = bounds[keys.index(key) :][:2]
        gate, up, sig, silu = swiglu_terms(gate_ring[lower:upper], up_ring[lower:upper])
        first = jnp.where(core == 0, whole, theirs)
        second = jnp.where(core == 0, theirs, whole)
        hidden = jnp.concatenate([first, second], axis=0).astype(F32)
        gate_grad = (hidden * up * sig * (1.0 + gate * (1.0 - sig))).astype(BF16)
        up_grad = (hidden * silu).astype(BF16)
        gate_grads[key], up_grads[key] = lax.optimization_barrier((gate_grad, up_grad))
        blocks = [[gate_grads[key]], [up_grads[key]]]
        terms[key] = product(blocks, [w_gate, w_up], "input_terms")
        return terms[key]

    mixed = {0: mixed_in}
    back, ahead = after((mixed_in, mixed_in), last_up, last_down)
    gate_ring, up_ring = collect(gates, ups, where, size)
    items = [None] + sequence[1:] + [1]
    for step, item in enumerate(items, 1):
        if step > 1:
            back, ahead = after((mixed[1 - step], mixed[step - 1]), *hold)
            mixed[1 - step], mixed[step - 1] = (back, ahead)
        if step < half:
            mixed[-step], mixed[step] = (ring.to_up(back), ring.to_down(ahead))
        else:
            last_up = ring.to_up(back[: rows // 2])
            last_down = ring.to_down(ahead[rows // 2 :])
        if step <= len(sequence):
            key = sequence[step - 1]
            shifts[key] = after(shifts[key], back, ahead)
            whole = sum_group(key)
            if step == len(sequence) - 1:
                far_rows = after((grads[half], far_part), back, ahead)
                part = jnp.concatenate([hidden_part(far_rows[:1]), far_rows[1]], axis=0)
                pairs[half] = pair_sum(part)
            if step < len(sequence):
                send_group(sequence[step], whole)
        hold = (finish_group(item),) if item else (gate_ring, up_ring)
    last_up, last_down = after((last_up, last_down), *hold)
    mixed[half] = jnp.concatenate([last_up, last_down], axis=0)
    mixed_parts = [mixed[d] for d in order]

    far_term = after(terms[half], last_up, last_down)
    sent_up = ring.to_up(far_term[: rows // 2])
    sent_down = ring.to_down(far_term[rows // 2 : rows])
    _, up, _, silu = swiglu_terms(*after((gate_ring, up_ring), far_term))
    act = (silu * up).astype(BF16)
    sent_up, sent_down = after((sent_up, sent_down), act)
    going_up = add(far_term[rows : 2 * rows], jnp.pad(sent_up, ((0, rows // 2), (0, 0))))
    going_down = add(far_term[2 * rows :], jnp.pad(sent_down, ((rows // 2, 0), (0, 0))))
    sent_up, sent_down = (ring.to_up(going_up), ring.to_down(going_down))
    gate_parts = after([gate_grads[key] for key in keys], going_up, going_down)
    gate_wgrad = wgrad(mixed_parts, gate_parts, "gate_wgrad")
    hold = (gate_wgrad,)
    for key in keys[1:]:
        sent_up, sent_down = after((sent_up, sent_down), *hold)
        going_up = add(terms[key][:rows], sent_up)
        going_down = add(terms[key][rows : 2 * rows], sent_down)
        sent_up, sent_down = (ring.to_up(going_up), ring.to_down(going_down))
        hold = ()
        if key == keys[1]:
            up_parts = after([up_grads[key] for key in keys], going_up, going_down)
            up_wgrad = wgrad(mixed_parts, up_parts, "up_wgrad")
            hold = (up_wgrad,)
        if key == keys[-1]:
            act = after(act, going_up, going_down)
            down_wgrad = wgrad([act], grad_parts, "down_wgrad")
    sent_up, sent_down = after((sent_up, sent_down), down_wgrad)
    mlp_grad = terms[1][2 * rows :].astype(F32) + sent_up.astype(F32) + sent_down.astype(F32)

    total_grad = out_grad.astype(F32) + mlp_grad.reshape(planes, height, breadth, features)
    rounded = total_grad.astype(BF16)
    before, beyond = neighbour_planes(rounded, "row")
    kernel_grad = sum_over(tap_sums(total_grad, framed_in), "row").reshape(conv_kernel.shape)
    grad_rimmed = jnp.concatenate([before, rounded, beyond], axis=0).astype(F32)
    patch_grad = (total_grad + correlate(frame_sides(grad_rimmed), conv_kernel, True)).astype(BF16)
    return (patch_grad, kernel_grad, gate_wgrad, up_wgrad, down_wgrad)


def solution(mesh):
    return jax.shard_map(
        body,
        mesh=mesh,
        in_specs=(
            P("row", None, None, "col"),
            P("row", None, None, "col"),
            P(None, None, None, "col"),
            P("col", "row"),
            P("col", "row"),
            P("col", "row"),
            P("col", "row"),
            P("row", "col"),
        ),
        out_specs=(
            P("row", None, None, "col"),
            P(None, None, None, "col"),
            P("col", "row"),
            P("col", "row"),
            P("row", "col"),
        ),
        check_vma=False,
    )
```

```python
import functools

import jax
import jax.numpy as jnp
import numpy as np
from jax import lax
from jax.experimental import pallas as pl
from jax.experimental.pallas import tpu as pltpu
from jax.sharding import PartitionSpec as P

F32 = jnp.float32
BF16 = jnp.bfloat16
CONTRACT_COLS = (((1,), (1,)), ((), ()))
CONTRACT_ROWS = (((0,), (0,)), ((), ()))


def dot(a, b, dims):
    return lax.dot_general(a, b, dims, preferred_element_type=F32)


def after(values, *earlier):
    return lax.optimization_barrier((values, earlier))[0]


def ring_order(peers):
    return list(range(0, peers, 2)) + list(range(1, peers, 2))[::-1]


class Ring:
    def __init__(self, axis):
        self.axis = axis
        self.size = lax.axis_size(axis)
        self.order = ring_order(self.size)
        self.up = [(self.order[i], self.order[(i + 1) % self.size]) for i in range(self.size)]
        self.down = [(j, i) for i, j in self.up]

    def neighbour(self, index, distance):
        return self.order[(self.order.index(index) + distance) % self.size]

    def to_up(self, x):
        return lax.ppermute(x, self.axis, self.up)

    def to_down(self, x):
        return lax.ppermute(x, self.axis, self.down)


def neighbour_planes(x, axis):
    peers = lax.axis_size(axis)
    up = [(i, (i + 1) % peers) for i in range(peers - 1)]
    down = [(j, i) for i, j in up]
    return (lax.ppermute(x[-1:], axis, up), lax.ppermute(x[:1], axis, down))


def correlate(framed, kernel, flipped):
    planes, height, breadth = (n - 2 for n in framed.shape[:3])
    summed = jnp.zeros((planes, height, breadth, framed.shape[3]), F32)
    for along_z in range(3):
        for along_y in range(3):
            for along_x in range(3):
                if flipped:
                    lead_z, lead_y, lead_x = (2 - along_z, 2 - along_y, 2 - along_x)
                else:
                    lead_z, lead_y, lead_x = (along_z, along_y, along_x)
                window = framed[
                    lead_z : lead_z + planes, lead_y : lead_y + height, lead_x : lead_x + breadth
                ]
                summed = summed + kernel[along_z, along_y, along_x] * window
    return summed


def frame_sides(field):
    return jnp.pad(field, ((0, 0), (1, 1), (1, 1), (0, 0)))


def tap_sums(grads, framed):
    planes, height, breadth = grads.shape[:3]
    layers = []
    for along_z in range(3):
        for along_y in range(3):
            for along_x in range(3):
                window = framed[
                    along_z : along_z + planes,
                    along_y : along_y + height,
                    along_x : along_x + breadth,
                ]
                layers.append(jnp.sum(grads * window, axis=(0, 1, 2)))
    return jnp.stack(layers)


def sum_over(x, axis, *earlier):
    peers = lax.axis_size(axis)
    if peers & (peers - 1):
        return lax.psum(x.astype(BF16), axis).astype(F32)
    reach = 1
    while reach < peers:
        mine = x.astype(BF16)
        theirs = lax.ppermute(mine, axis, [(i, i ^ reach) for i in range(peers)])
        reach *= 2
        if reach == peers:
            theirs = after(theirs, *earlier)
        x = mine.astype(F32) + theirs.astype(F32)
    return x


def swap_cores(x):
    peers = lax.axis_size("col")
    return lax.ppermute(x, "col", [(i, i ^ 1) for i in range(peers)])


def shift_chips(x, count):
    peers = lax.axis_size("col")
    return lax.ppermute(x, "col", [(i, (i + 2 * count) % peers) for i in range(peers)])


def col_place(me, block, chips):
    other = 0 if me % 2 == block % 2 else 1
    return other * chips + (me // 2 - block // 2) % chips


def piece_table(ring, distances, rows, col_rows, size):
    peers, cols = (ring.size, lax.axis_size("col"))
    table = np.zeros((peers, cols, 2, len(distances) * rows // size), np.int32)
    for row in range(peers):
        starts = [
            ring.neighbour(row, d) * rows + at for d in distances for at in range(0, rows, size)
        ]
        for col in range(cols):
            table[row, col, 0] = [col_place(col, s // col_rows, cols // 2) for s in starts]
            table[row, col, 1] = [s % col_rows for s in starts]
    return jnp.asarray(table)[lax.axis_index("row"), lax.axis_index("col")]


def split_halves(x, core):
    rows = x.shape[0] // 2
    x = x.astype(BF16)
    keep = jnp.where(core == 0, x[:rows], x[rows:])
    give = jnp.where(core == 0, x[rows:], x[:rows])
    return (keep, give)


def add(*terms):
    total = terms[0].astype(F32)
    for term in terms[1:]:
        total = total + term.astype(F32)
    return total.astype(BF16)


LIGHT = pl.CostEstimate(flops=0, bytes_accessed=0, transcendentals=0)


def product_kernel(tokens, weights, refs):
    out = refs[-1]
    total = None
    for n in range(weights):
        rows = [ref[...] for ref in refs[n * tokens : (n + 1) * tokens]]
        rows = rows[0] if tokens == 1 else jnp.concatenate(rows, axis=0)
        term = dot(rows, refs[weights * tokens + n][...], CONTRACT_COLS)
        total = term if total is None else total + term
    out[...] = total.astype(out.dtype)


def product(blocks, weights, name):
    tokens = len(blocks[0])
    rows = sum(block.shape[0] for block in blocks[0])
    wide, depth = weights[0].shape
    tile = next(t for t in (896 if len(weights) == 1 else 512, 512, 256, 128) if wide % t == 0)
    flat = [block for group in blocks for block in group]
    return pl.pallas_call(
        lambda *refs: product_kernel(tokens, len(weights), refs),
        grid=(wide // tile,),
        out_shape=jax.ShapeDtypeStruct((rows, wide), BF16),
        in_specs=[pl.BlockSpec(block.shape, lambda i: (0, 0)) for block in flat]
        + [pl.BlockSpec((tile, depth), lambda i: (i, 0))] * len(weights),
        out_specs=pl.BlockSpec((rows, tile), lambda i: (0, i)),
        compiler_params=pltpu.CompilerParams(vmem_limit_bytes=18 << 20),
        cost_estimate=LIGHT,
        name=name,
    )(*flat, *weights)


def collect_kernel(sources, count, size, where_ref, *refs):
    inputs, outputs, sems = (refs[:sources], refs[sources : sources + 2], refs[-1])
    rows = inputs[0].shape[0] // 2

    def copies(source, piece, offset):
        place = pl.ds(piece * size, size)
        return [
            pltpu.make_async_copy(
                inputs[source].at[pl.ds(pl.multiple_of(offset + n * rows, size), size)],
                outputs[n].at[place],
                sems.at[n, piece],
            )
            for n in range(2)
        ]

    for piece in range(count):
        for source in range(sources):

            @pl.when(where_ref[0, piece] == source)
            def _():
                for copy in copies(source, piece, where_ref[1, piece]):
                    copy.start()

    for piece in range(count):
        for copy in copies(0, piece, 0):
            copy.wait()


def collect(pairs, where, size):
    sources, count, width = (len(pairs), where.shape[1], pairs[0].shape[1])
    shape = jax.ShapeDtypeStruct((count * size, width), BF16)
    anywhere = pl.BlockSpec(memory_space=pl.ANY)
    return pl.pallas_call(
        functools.partial(collect_kernel, sources, count, size),
        out_shape=[shape] * 2,
        in_specs=[pl.BlockSpec(memory_space=pltpu.SMEM)] + [anywhere] * sources,
        out_specs=[anywhere] * 2,
        scratch_shapes=[pltpu.SemaphoreType.DMA((2, count))],
        compiler_params=pltpu.CompilerParams(vmem_limit_bytes=1 << 20),
        cost_estimate=LIGHT,
        name="collect_gate_up",
    )(where, *pairs)


def swiglu_terms(gate, up):
    gate, up = (gate.astype(F32), up.astype(F32))
    sig = jax.nn.sigmoid(gate)
    return (gate, up, sig, gate * sig)


def wgrad_kernel(spans_a, spans_b, tile, a_refs, b_refs, out, a_buf, b_buf, a_sems, b_sems):
    step = pl.program_id(0)
    tiles = a_buf.shape[1] // tile

    def a_copies(t):
        columns = pl.ds(t * tile, tile)
        return [
            pltpu.make_async_copy(
                ref.at[:, columns], a_buf.at[pl.ds(at, rows), columns], a_sems.at[t, n]
            )
            for n, (ref, (at, rows)) in enumerate(zip(a_refs, spans_a))
        ]

    def b_copies():
        return [
            pltpu.make_async_copy(ref, b_buf.at[pl.ds(at, rows)], b_sems.at[n])
            for n, (ref, (at, rows)) in enumerate(zip(b_refs, spans_b))
        ]

    @pl.when(step == 0)
    def _():
        for copy in a_copies(0) + b_copies():
            copy.start()
        for t in range(1, tiles):
            for copy in a_copies(t):
                copy.start()
        for copy in b_copies():
            copy.wait()

    for t in range(tiles):

        @pl.when(step == t)
        def _():
            for copy in a_copies(t):
                copy.wait()
            out[...] = dot(
                a_buf[:, t * tile : (t + 1) * tile], b_buf[...], CONTRACT_ROWS
            ).astype(out.dtype)


def spans(parts):
    at, found = (0, [])
    for part in parts:
        found.append((at, part.shape[0]))
        at += part.shape[0]
    return found


def wgrad(a_parts, b_parts, name):
    depth = sum(part.shape[0] for part in a_parts)
    wide, high = (b_parts[0].shape[1], a_parts[0].shape[1])
    tile = next(t for t in (512, 256, 128) if high % t == 0)
    n_a, n_b = (len(a_parts), len(b_parts))

    def kernel(*refs):
        wgrad_kernel(
            spans(a_parts), spans(b_parts), tile, refs[:n_a], refs[n_a : n_a + n_b], *refs[n_a + n_b :]
        )

    return pl.pallas_call(
        kernel,
        grid=(high // tile,),
        out_shape=pltpu.HBM((high, wide), BF16),
        in_specs=[pl.BlockSpec(memory_space=pltpu.HBM)] * (n_a + n_b),
        out_specs=pl.BlockSpec((tile, wide), lambda i: (i, 0)),
        scratch_shapes=[
            pltpu.VMEM((depth, high), BF16),
            pltpu.VMEM((depth, wide), BF16),
            pltpu.SemaphoreType.DMA((high // tile, n_a)),
            pltpu.SemaphoreType.DMA((n_b,)),
        ],
        compiler_params=pltpu.CompilerParams(vmem_limit_bytes=20 << 20),
        cost_estimate=LIGHT,
        name=name,
    )(*a_parts, *b_parts)


def body(patches, out_grad, conv_kernel, saved_gate, saved_up, w_gate, w_up, w_down):
    planes, height, breadth, features = patches.shape
    ring = Ring("row")
    half = ring.size // 2
    rows = planes * height * breadth
    chips = lax.axis_size("col") // 2
    core = lax.rem(lax.axis_index("col"), 2)
    flat_grad = out_grad.reshape(rows, features)

    far = [half, half - 1, 1 - half]
    near = [1, -1, 0]
    middle = [[d, -d] for d in range(half - 2, 1, -1)]
    groups = [far] + middle + [near]
    order = [d for group in groups for d in group]
    bounds = np.cumsum([0] + [len(group) * rows for group in groups])
    col_rows = saved_gate.shape[0]
    size = int(np.gcd(rows, col_rows))
    where = piece_table(ring, order, rows, col_rows, size)

    def hidden_part(blocks):
        return product([blocks], [w_down], "hidden_grad")

    def pair_sum(partial):
        keep, give = split_halves(partial, core)
        return add(keep, swap_cores(give))

    def chip_shifts(x):
        return [shift_chips(x, k) for k in range(1, chips)]

    keys = [half] + [group[0] for group in middle] + [1]
    sequence = keys[1:-1][::-1] + [half, 1]
    pairs, shifts, halves = ({}, {}, {})

    def sum_group(key):
        whole = add(pairs[key], *shifts[key])
        halves[key] = (whole, swap_cores(whole))

    def send_group(key):
        shifts[key] = chip_shifts(pairs[key])

    before, beyond = neighbour_planes(patches, "row")
    grads = {0: flat_grad}
    grads[-1], grads[1] = (ring.to_up(flat_grad), ring.to_down(flat_grad))
    saved = jnp.concatenate([saved_gate, saved_up], axis=0)
    saved = [saved] + chip_shifts(saved)
    hold = ()
    for step in range(2, half + 1):
        back, ahead = after((grads[1 - step], grads[step - 1]), *hold)
        grads[1 - step], grads[step - 1] = (back, ahead)
        if step < half:
            grads[-step], grads[step] = (ring.to_up(back), ring.to_down(ahead))
        else:
            last_up = ring.to_up(back[: rows // 2])
            last_down = ring.to_down(ahead[rows // 2 :])
        if step == 2:
            part = hidden_part([ahead, back, flat_grad])
            pairs[1] = pair_sum(part)
            planes_in, before, beyond = after((patches, before, beyond), part)
            rimmed = jnp.concatenate([before, planes_in, beyond], axis=0)
            framed_in = frame_sides(rimmed.astype(F32))
            mixed_in = planes_in.astype(F32) + correlate(framed_in, conv_kernel, False)
            mixed_in = mixed_in.astype(BF16).reshape(rows, features)
            hold = (part, mixed_in, where)
        elif step < half:
            part = hidden_part([ahead, back])
            pairs[step - 1] = pair_sum(part)
            send_group(step - 1)
            hold = (part, pairs[1])
        else:
            far_part = hidden_part([ahead, back])
            hold = (far_part, pairs[step - 2])
    last_up, last_down = after((last_up, last_down), *hold)
    grads[half] = jnp.concatenate([last_up, last_down], axis=0)
    grad_parts = [grads[d] for d in order]

    gate_grads, up_grads, terms = ({}, {}, {})

    def finish_group(key):
        whole, theirs = halves[key]
        lower, upper = bounds[keys.index(key) :][:2]
        gate, up, sig, silu = swiglu_terms(gate_ring[lower:upper], up_ring[lower:upper])
        first = jnp.where(core == 0, whole, theirs)
        second = jnp.where(core == 0, theirs, whole)
        hidden = jnp.concatenate([first, second], axis=0).astype(F32)
        gate_grad = (hidden * up * sig * (1.0 + gate * (1.0 - sig))).astype(BF16)
        up_grad = (hidden * silu).astype(BF16)
        gate_grads[key], up_grads[key] = lax.optimization_barrier((gate_grad, up_grad))
        blocks = [[gate_grads[key]], [up_grads[key]]]
        terms[key] = product(blocks, [w_gate, w_up], "input_terms")
        return terms[key]

    mixed = {0: mixed_in}
    back, ahead = after((mixed_in, mixed_in), last_up, last_down)
    saved = after(saved, last_up, last_down)
    saved += [swap_cores(x) for x in saved]
    gate_ring, up_ring = collect(saved, where, size)
    items = [None] + sequence[:-2] + ["down", half]
    for step, item in enumerate(items, 1):
        if step > 1:
            back, ahead = after((mixed[1 - step], mixed[step - 1]), *hold)
            mixed[1 - step], mixed[step - 1] = (back, ahead)
        if step < half:
            mixed[-step], mixed[step] = (ring.to_up(back), ring.to_down(ahead))
        else:
            last_up = ring.to_up(back[: rows // 2])
            last_down = ring.to_down(ahead[rows // 2 :])
        if step == 1:
            far_rows = after((grads[half], far_part), saved[-1])
            part = jnp.concatenate([hidden_part(far_rows[:1]), far_rows[1]], axis=0)
            pairs[half] = pair_sum(part)
            send_group(half)
            pairs[1] = after(pairs[1], gate_ring, *shifts[sequence[0]])
            send_group(1)
        if item is None:
            hold = (gate_ring, up_ring)
        elif item == "down":
            _, up, _, silu = swiglu_terms(*after((gate_ring, up_ring), back, ahead, *shifts[1]))
            down_wgrad = wgrad([(silu * up).astype(BF16)], grad_parts, "down_wgrad")
            hold = (down_wgrad,)
            shifts[half] = after(shifts[half], down_wgrad)
        else:
            shifts[item] = after(shifts[item], back, ahead)
            sum_group(item)
            hold = (finish_group(item),)
    last_up, last_down = after((last_up, last_down), *hold)
    mixed[half] = jnp.concatenate([last_up, last_down], axis=0)
    mixed_parts = [mixed[d] for d in order]

    far_term = after(terms[half], last_up, last_down)
    sent_up = ring.to_up(far_term[: rows // 2])
    sent_down = ring.to_down(far_term[rows // 2 : rows])
    shifts[1] = after(shifts[1], last_up, last_down)
    sum_group(1)
    sent_up, sent_down = after((sent_up, sent_down), finish_group(1))
    going_up = add(far_term[rows : 2 * rows], jnp.pad(sent_up, ((0, rows // 2), (0, 0))))
    going_down = add(far_term[2 * rows :], jnp.pad(sent_down, ((rows // 2, 0), (0, 0))))
    sent_up, sent_down = (ring.to_up(going_up), ring.to_down(going_down))
    gate_parts = after([gate_grads[key] for key in keys], going_up, going_down)
    gate_wgrad = wgrad(mixed_parts, gate_parts, "gate_wgrad")
    hold = (gate_wgrad,)
    for key in keys[1:]:
        sent_up, sent_down = after((sent_up, sent_down), *hold)
        going_up = add(terms[key][:rows], sent_up)
        going_down = add(terms[key][rows : 2 * rows], sent_down)
        sent_up, sent_down = (ring.to_up(going_up), ring.to_down(going_down))
        hold = ()
        if key == keys[1]:
            up_parts = after([up_grads[key] for key in keys], going_up, going_down)
            up_wgrad = wgrad(mixed_parts, up_parts, "up_wgrad")
            hold = (up_wgrad,)
    mlp_grad = terms[1][2 * rows :].astype(F32) + sent_up.astype(F32) + sent_down.astype(F32)

    total_grad = out_grad.astype(F32) + mlp_grad.reshape(planes, height, breadth, features)
    rounded = total_grad.astype(BF16)
    before, beyond = neighbour_planes(rounded, "row")
    grad_rimmed = jnp.concatenate([before, rounded, beyond], axis=0).astype(F32)
    patch_grad = (total_grad + correlate(frame_sides(grad_rimmed), conv_kernel, True)).astype(BF16)
    kernel_grad = sum_over(tap_sums(total_grad, framed_in), "row", patch_grad)
    kernel_grad = kernel_grad.reshape(conv_kernel.shape)
    return (patch_grad, kernel_grad, gate_wgrad, up_wgrad, down_wgrad)


def solution(mesh):
    return jax.shard_map(
        body,
        mesh=mesh,
        in_specs=(
            P("row", None, None, "col"),
            P("row", None, None, "col"),
            P(None, None, None, "col"),
            P("col", "row"),
            P("col", "row"),
            P("col", "row"),
            P("col", "row"),
            P("row", "col"),
        ),
        out_specs=(
            P("row", None, None, "col"),
            P(None, None, None, "col"),
            P("col", "row"),
            P("col", "row"),
            P("row", "col"),
        ),
        check_vma=False,
    )
```

```python
import functools

import jax
import jax.numpy as jnp
import numpy as np
from jax import lax
from jax.experimental import pallas as pl
from jax.experimental.pallas import tpu as pltpu
from jax.sharding import PartitionSpec as P

F32 = jnp.float32
BF16 = jnp.bfloat16
CONTRACT_COLS = (((1,), (1,)), ((), ()))
CONTRACT_ROWS = (((0,), (0,)), ((), ()))


def dot(a, b, dims):
    return lax.dot_general(a, b, dims, preferred_element_type=F32)


def after(values, *earlier):
    return lax.optimization_barrier((values, earlier))[0]


def ring_order(peers):
    return list(range(0, peers, 2)) + list(range(1, peers, 2))[::-1]


class Ring:
    def __init__(self, axis):
        self.axis = axis
        self.size = lax.axis_size(axis)
        self.order = ring_order(self.size)
        self.up = [(self.order[i], self.order[(i + 1) % self.size]) for i in range(self.size)]
        self.down = [(j, i) for i, j in self.up]

    def neighbour(self, index, distance):
        return self.order[(self.order.index(index) + distance) % self.size]

    def to_up(self, x):
        return lax.ppermute(x, self.axis, self.up)

    def to_down(self, x):
        return lax.ppermute(x, self.axis, self.down)


def neighbour_planes(x, axis):
    peers = lax.axis_size(axis)
    up = [(i, (i + 1) % peers) for i in range(peers - 1)]
    down = [(j, i) for i, j in up]
    return (lax.ppermute(x[-1:], axis, up), lax.ppermute(x[:1], axis, down))


def correlate(framed, kernel, flipped):
    planes, height, breadth = (n - 2 for n in framed.shape[:3])
    summed = jnp.zeros((planes, height, breadth, framed.shape[3]), F32)
    for along_z in range(3):
        for along_y in range(3):
            for along_x in range(3):
                if flipped:
                    lead_z, lead_y, lead_x = (2 - along_z, 2 - along_y, 2 - along_x)
                else:
                    lead_z, lead_y, lead_x = (along_z, along_y, along_x)
                window = framed[
                    lead_z : lead_z + planes, lead_y : lead_y + height, lead_x : lead_x + breadth
                ]
                summed = summed + kernel[along_z, along_y, along_x] * window
    return summed


def frame_sides(field):
    return jnp.pad(field, ((0, 0), (1, 1), (1, 1), (0, 0)))


def tap_sums(grads, framed):
    planes, height, breadth = grads.shape[:3]
    layers = []
    for along_z in range(3):
        for along_y in range(3):
            for along_x in range(3):
                window = framed[
                    along_z : along_z + planes,
                    along_y : along_y + height,
                    along_x : along_x + breadth,
                ]
                layers.append(jnp.sum(grads * window, axis=(0, 1, 2)))
    return jnp.stack(layers)


def sum_over(x, axis, *earlier):
    peers = lax.axis_size(axis)
    if peers & (peers - 1):
        return lax.psum(x.astype(BF16), axis).astype(F32)
    reach = 1
    while reach < peers:
        mine = x.astype(BF16)
        theirs = lax.ppermute(mine, axis, [(i, i ^ reach) for i in range(peers)])
        reach *= 2
        if reach == peers:
            theirs = after(theirs, *earlier)
        x = mine.astype(F32) + theirs.astype(F32)
    return x


def swap_cores(x):
    peers = lax.axis_size("col")
    return lax.ppermute(x, "col", [(i, i ^ 1) for i in range(peers)])


def shift_chips(x, count):
    peers = lax.axis_size("col")
    return lax.ppermute(x, "col", [(i, (i + 2 * count) % peers) for i in range(peers)])


def col_place(me, block, chips):
    other = 0 if me % 2 == block % 2 else 1
    return other * chips + (me // 2 - block // 2) % chips


def piece_table(ring, distances, rows, col_rows, size):
    peers, cols = (ring.size, lax.axis_size("col"))
    table = np.zeros((peers, cols, 2, len(distances) * rows // size), np.int32)
    for row in range(peers):
        starts = [
            ring.neighbour(row, d) * rows + at for d in distances for at in range(0, rows, size)
        ]
        for col in range(cols):
            table[row, col, 0] = [col_place(col, s // col_rows, cols // 2) for s in starts]
            table[row, col, 1] = [s % col_rows for s in starts]
    return jnp.asarray(table)[lax.axis_index("row"), lax.axis_index("col")]


def split_halves(x, core):
    rows = x.shape[0] // 2
    x = x.astype(BF16)
    keep = jnp.where(core == 0, x[:rows], x[rows:])
    give = jnp.where(core == 0, x[rows:], x[:rows])
    return (keep, give)


def add(*terms):
    total = terms[0].astype(F32)
    for term in terms[1:]:
        total = total + term.astype(F32)
    return total.astype(BF16)


LIGHT = pl.CostEstimate(flops=0, bytes_accessed=0, transcendentals=0)


def product_kernel(tokens, weights, refs):
    out = refs[-1]
    total = None
    for n in range(weights):
        rows = [ref[...] for ref in refs[n * tokens : (n + 1) * tokens]]
        rows = rows[0] if tokens == 1 else jnp.concatenate(rows, axis=0)
        term = dot(rows, refs[weights * tokens + n][...], CONTRACT_COLS)
        total = term if total is None else total + term
    out[...] = total.astype(out.dtype)


def product(blocks, weights, name):
    tokens = len(blocks[0])
    rows = sum(block.shape[0] for block in blocks[0])
    wide, depth = weights[0].shape
    tile = next(t for t in (896 if len(weights) == 1 else 512, 512, 256, 128) if wide % t == 0)
    flat = [block for group in blocks for block in group]
    return pl.pallas_call(
        lambda *refs: product_kernel(tokens, len(weights), refs),
        grid=(wide // tile,),
        out_shape=jax.ShapeDtypeStruct((rows, wide), BF16),
        in_specs=[pl.BlockSpec(block.shape, lambda i: (0, 0)) for block in flat]
        + [pl.BlockSpec((tile, depth), lambda i: (i, 0))] * len(weights),
        out_specs=pl.BlockSpec((rows, tile), lambda i: (0, i)),
        compiler_params=pltpu.CompilerParams(vmem_limit_bytes=18 << 20),
        cost_estimate=LIGHT,
        name=name,
    )(*flat, *weights)


def collect_kernel(sources, count, size, where_ref, *refs):
    inputs, outputs, sems = (refs[:sources], refs[sources : sources + 2], refs[-1])
    rows = inputs[0].shape[0] // 2

    def copies(source, piece, offset):
        place = pl.ds(piece * size, size)
        return [
            pltpu.make_async_copy(
                inputs[source].at[pl.ds(pl.multiple_of(offset + n * rows, size), size)],
                outputs[n].at[place],
                sems.at[n, piece],
            )
            for n in range(2)
        ]

    for piece in range(count):
        for source in range(sources):

            @pl.when(where_ref[0, piece] == source)
            def _():
                for copy in copies(source, piece, where_ref[1, piece]):
                    copy.start()

    for piece in range(count):
        for copy in copies(0, piece, 0):
            copy.wait()


def collect(pairs, where, size):
    sources, count, width = (len(pairs), where.shape[1], pairs[0].shape[1])
    shape = jax.ShapeDtypeStruct((count * size, width), BF16)
    anywhere = pl.BlockSpec(memory_space=pl.ANY)
    return pl.pallas_call(
        functools.partial(collect_kernel, sources, count, size),
        out_shape=[shape] * 2,
        in_specs=[pl.BlockSpec(memory_space=pltpu.SMEM)] + [anywhere] * sources,
        out_specs=[anywhere] * 2,
        scratch_shapes=[pltpu.SemaphoreType.DMA((2, count))],
        compiler_params=pltpu.CompilerParams(vmem_limit_bytes=1 << 20),
        cost_estimate=LIGHT,
        name="collect_gate_up",
    )(where, *pairs)


def swiglu_terms(gate, up):
    gate, up = (gate.astype(F32), up.astype(F32))
    sig = jax.nn.sigmoid(gate)
    return (gate, up, sig, gate * sig)


def wgrad_kernel(spans_a, spans_b, tile, a_refs, b_refs, out, a_buf, b_buf, a_sems, b_sems):
    step = pl.program_id(0)
    tiles = a_buf.shape[1] // tile

    def a_copies(t):
        columns = pl.ds(t * tile, tile)
        return [
            pltpu.make_async_copy(
                ref.at[:, columns], a_buf.at[pl.ds(at, rows), columns], a_sems.at[t, n]
            )
            for n, (ref, (at, rows)) in enumerate(zip(a_refs, spans_a))
        ]

    def b_copies():
        return [
            pltpu.make_async_copy(ref, b_buf.at[pl.ds(at, rows)], b_sems.at[n])
            for n, (ref, (at, rows)) in enumerate(zip(b_refs, spans_b))
        ]

    @pl.when(step == 0)
    def _():
        for copy in a_copies(0) + b_copies():
            copy.start()
        for t in range(1, tiles):
            for copy in a_copies(t):
                copy.start()
        for copy in b_copies():
            copy.wait()

    for t in range(tiles):

        @pl.when(step == t)
        def _():
            for copy in a_copies(t):
                copy.wait()
            out[...] = dot(
                a_buf[:, t * tile : (t + 1) * tile], b_buf[...], CONTRACT_ROWS
            ).astype(out.dtype)


def spans(parts):
    at, found = (0, [])
    for part in parts:
        found.append((at, part.shape[0]))
        at += part.shape[0]
    return found


def wgrad(a_parts, b_parts, name):
    depth = sum(part.shape[0] for part in a_parts)
    wide, high = (b_parts[0].shape[1], a_parts[0].shape[1])
    tile = next(t for t in (512, 256, 128) if high % t == 0)
    n_a, n_b = (len(a_parts), len(b_parts))

    def kernel(*refs):
        wgrad_kernel(
            spans(a_parts), spans(b_parts), tile, refs[:n_a], refs[n_a : n_a + n_b], *refs[n_a + n_b :]
        )

    return pl.pallas_call(
        kernel,
        grid=(high // tile,),
        out_shape=pltpu.HBM((high, wide), BF16),
        in_specs=[pl.BlockSpec(memory_space=pltpu.HBM)] * (n_a + n_b),
        out_specs=pl.BlockSpec((tile, wide), lambda i: (i, 0)),
        scratch_shapes=[
            pltpu.VMEM((depth, high), BF16),
            pltpu.VMEM((depth, wide), BF16),
            pltpu.SemaphoreType.DMA((high // tile, n_a)),
            pltpu.SemaphoreType.DMA((n_b,)),
        ],
        compiler_params=pltpu.CompilerParams(vmem_limit_bytes=20 << 20),
        cost_estimate=LIGHT,
        name=name,
    )(*a_parts, *b_parts)


def body(patches, out_grad, conv_kernel, saved_gate, saved_up, w_gate, w_up, w_down):
    planes, height, breadth, features = patches.shape
    ring = Ring("row")
    half = ring.size // 2
    rows = planes * height * breadth
    chips = lax.axis_size("col") // 2
    core = lax.rem(lax.axis_index("col"), 2)
    flat_grad = out_grad.reshape(rows, features)

    far = [half, half - 1, 1 - half]
    near = [1, -1, 0]
    middle = [[d, -d] for d in range(half - 2, 1, -1)]
    groups = [far] + middle + [near]
    order = [d for group in groups for d in group]
    bounds = np.cumsum([0] + [len(group) * rows for group in groups])
    col_rows = saved_gate.shape[0]
    size = int(np.gcd(rows, col_rows))
    where = piece_table(ring, order, rows, col_rows, size)

    def hidden_part(blocks):
        return product([blocks], [w_down], "hidden_grad")

    def pair_sum(partial):
        keep, give = split_halves(partial, core)
        return add(keep, swap_cores(give))

    def chip_shifts(x):
        return [shift_chips(x, k) for k in range(1, chips)]

    keys = [half] + [group[0] for group in middle] + [1]
    sequence = keys[1:-1][::-1] + [half, 1]
    pairs, shifts, halves = ({}, {}, {})

    def sum_group(key):
        whole = add(pairs[key], *shifts[key])
        halves[key] = (whole, swap_cores(whole))

    def send_group(key):
        shifts[key] = chip_shifts(pairs[key])

    before, beyond = neighbour_planes(patches, "row")
    grads = {0: flat_grad}
    grads[-1], grads[1] = (ring.to_up(flat_grad), ring.to_down(flat_grad))
    saved = jnp.concatenate([saved_gate, saved_up], axis=0)
    saved = [saved] + chip_shifts(saved)
    hold = ()
    for step in range(2, half + 1):
        back, ahead = after((grads[1 - step], grads[step - 1]), *hold)
        grads[1 - step], grads[step - 1] = (back, ahead)
        if step < half:
            grads[-step], grads[step] = (ring.to_up(back), ring.to_down(ahead))
        else:
            last_up = ring.to_up(back[: rows // 2])
            last_down = ring.to_down(ahead[rows // 2 :])
        if step == 2:
            part = hidden_part([ahead, back, flat_grad])
            pairs[1] = pair_sum(part)
            planes_in, before, beyond = after((patches, before, beyond), part)
            rimmed = jnp.concatenate([before, planes_in, beyond], axis=0)
            framed_in = frame_sides(rimmed.astype(F32))
            mixed_in = planes_in.astype(F32) + correlate(framed_in, conv_kernel, False)
            mixed_in = mixed_in.astype(BF16).reshape(rows, features)
            hold = (part, mixed_in, where)
        elif step < half:
            part = hidden_part([ahead, back])
            pairs[step - 1] = pair_sum(part)
            send_group(step - 1)
            hold = (part, pairs[1])
        else:
            far_part = hidden_part([ahead, back])
            hold = (far_part, pairs[step - 2])
    last_up, last_down = after((last_up, last_down), *hold)
    grads[half] = jnp.concatenate([last_up, last_down], axis=0)
    grad_parts = [grads[d] for d in order]

    gate_grads, up_grads, terms = ({}, {}, {})

    def finish_group(key):
        whole, theirs = halves[key]
        lower, upper = bounds[keys.index(key) :][:2]
        gate, up, sig, silu = swiglu_terms(gate_ring[lower:upper], up_ring[lower:upper])
        first = jnp.where(core == 0, whole, theirs)
        second = jnp.where(core == 0, theirs, whole)
        hidden = jnp.concatenate([first, second], axis=0).astype(F32)
        gate_grad = (hidden * up * sig * (1.0 + gate * (1.0 - sig))).astype(BF16)
        up_grad = (hidden * silu).astype(BF16)
        gate_grads[key], up_grads[key] = lax.optimization_barrier((gate_grad, up_grad))
        blocks = [[gate_grads[key]], [up_grads[key]]]
        terms[key] = product(blocks, [w_gate, w_up], "input_terms")
        return terms[key]

    mixed = {0: mixed_in}
    back, ahead = after((mixed_in, mixed_in), last_up, last_down)
    saved = after(saved, last_up, last_down)
    saved += [swap_cores(x) for x in saved]
    gate_ring, up_ring = collect(saved, where, size)
    items = [None] + sequence[:-2] + ["down", half]
    for step, item in enumerate(items, 1):
        if step > 1:
            back, ahead = after((mixed[1 - step], mixed[step - 1]), *hold)
            mixed[1 - step], mixed[step - 1] = (back, ahead)
        if step < half:
            mixed[-step], mixed[step] = (ring.to_up(back), ring.to_down(ahead))
        else:
            last_up = ring.to_up(back[: rows // 2])
            last_down = ring.to_down(ahead[rows // 2 :])
        if step == 1:
            far_rows = after((grads[half], far_part), saved[-1])
            part = jnp.concatenate([hidden_part(far_rows[:1]), far_rows[1]], axis=0)
            pairs[half] = pair_sum(part)
            send_group(half)
            pairs[1] = after(pairs[1], gate_ring, *shifts[sequence[0]])
            send_group(1)
        if item is None:
            hold = (gate_ring, up_ring)
        elif item == "down":
            _, up, _, silu = swiglu_terms(*after((gate_ring, up_ring), back, ahead, *shifts[1]))
            down_wgrad = wgrad([(silu * up).astype(BF16)], grad_parts, "down_wgrad")
            hold = (down_wgrad,)
            shifts[half] = after(shifts[half], down_wgrad)
        else:
            shifts[item] = after(shifts[item], back, ahead)
            sum_group(item)
            hold = (finish_group(item),)
    last_up, last_down = after((last_up, last_down), *hold)
    mixed[half] = jnp.concatenate([last_up, last_down], axis=0)
    mixed_parts = [mixed[d] for d in order]

    far_term = after(terms[half], last_up, last_down)
    sent_up = ring.to_up(far_term[: rows // 2])
    sent_down = ring.to_down(far_term[rows // 2 : rows])
    shifts[1] = after(shifts[1], last_up, last_down)
    sum_group(1)
    sent_up, sent_down = after((sent_up, sent_down), finish_group(1))
    going_up = add(far_term[rows : 2 * rows], jnp.pad(sent_up, ((0, rows // 2), (0, 0))))
    going_down = add(far_term[2 * rows :], jnp.pad(sent_down, ((rows // 2, 0), (0, 0))))
    sent_up, sent_down = (ring.to_up(going_up), ring.to_down(going_down))
    gate_parts = after([gate_grads[key] for key in keys], going_up, going_down)
    gate_wgrad = wgrad(mixed_parts, gate_parts, "gate_wgrad")
    hold = (gate_wgrad,)
    for key in keys[1:]:
        sent_up, sent_down = after((sent_up, sent_down), *hold)
        going_up = add(terms[key][:rows], sent_up)
        going_down = add(terms[key][rows : 2 * rows], sent_down)
        sent_up, sent_down = (ring.to_up(going_up), ring.to_down(going_down))
        hold = ()
        if key == keys[1]:
            up_parts = after([up_grads[key] for key in keys], going_up, going_down)
            up_wgrad = wgrad(mixed_parts, up_parts, "up_wgrad")
            hold = (up_wgrad,)
    mlp_grad = terms[1][2 * rows :].astype(F32) + sent_up.astype(F32) + sent_down.astype(F32)

    total_grad = out_grad.astype(F32) + mlp_grad.reshape(planes, height, breadth, features)
    rounded = total_grad.astype(BF16)
    before, beyond = neighbour_planes(rounded, "row")
    grad_rimmed = jnp.concatenate([before, rounded, beyond], axis=0).astype(F32)
    patch_grad = (total_grad + correlate(frame_sides(grad_rimmed), conv_kernel, True)).astype(BF16)
    taps = after(tap_sums(total_grad, framed_in), before, beyond)
    kernel_grad = sum_over(taps, "row", patch_grad)
    kernel_grad = kernel_grad.reshape(conv_kernel.shape)
    return (patch_grad, kernel_grad, gate_wgrad, up_wgrad, down_wgrad)


def solution(mesh):
    return jax.shard_map(
        body,
        mesh=mesh,
        in_specs=(
            P("row", None, None, "col"),
            P("row", None, None, "col"),
            P(None, None, None, "col"),
            P("col", "row"),
            P("col", "row"),
            P("col", "row"),
            P("col", "row"),
            P("row", "col"),
        ),
        out_specs=(
            P("row", None, None, "col"),
            P(None, None, None, "col"),
            P("col", "row"),
            P("col", "row"),
            P("row", "col"),
        ),
        check_vma=False,
    )
```
